256 devices in a mesh: mp: 2 (over y_lo), dp: 32 (over z, x), vocab: 4 (over y_hi, core).
Axes of the slice: x: 4, y: 4 (y_hi: 2, y_lo: 2; y = y_hi * 2 + y_lo), z: 8, core: 2. Of those that a mesh axis runs over, the one named last changes fastest.
Arguments:
- hidden_states: bfloat16 [2, 1024, 4096], P('mp', 'dp'), may hold values from -700 to 700
- head_weight: bfloat16 [2, 4096, 65536], P('mp', None, ('dp', 'vocab')), may hold values from -1 to 1
- targets: int32 [1024], replicated, may hold values from 0 to 65535
- train_step: int32 [1], replicated, may hold values from 0 to 999
Outputs:
- grad_hidden: float32 [2, 1024, 4096], P('mp', 'dp', 'vocab')
- grad_head: float32 [2, 4096, 65536], P('mp', None, ('dp', 'vocab'))
The draws below stay inside these ranges and needn't reach their ends.
All inputs are finite; a program needn't handle non-finite values.
Results may differ from the reference program's by a relative error of at most 0.0029.
Values may be sent and summed in bfloat16 or wider, within the bound.
No kernel may reach another device: no remote copies, remote signals or barrier semaphores. Data moves between devices by JAX's collectives and lax.ppermute only.
A program may use at most 128 MiB of HBM per device.

```python
import math
import jax
import jax.numpy as jnp
from jax import lax

D = 4096
VOCAB = 65536
WARMUP = 1000
TOKENS = 1024


aligned_rows = 4


def head_parts(key):
    key_noise, key_scale, key_pick = jax.random.split(key, 3)
    gauss_noise = jax.random.truncated_normal(key_noise, -6.0, 6.0, (2, D, VOCAB), jnp.float32)
    scales = jnp.exp(jax.random.uniform(key_scale, (2, 1, VOCAB), jnp.float32, math.log(0.75), math.log(7.5)))
    chosen = jnp.stack([jax.random.permutation(jax.random.fold_in(key_pick, index), VOCAB // 2)[:aligned_rows] for index in range(2)])
    pair_mark = jnp.zeros((2, VOCAB // 2), jnp.float32).at[jnp.arange(2)[:, None], chosen].set(1.0)
    even_cols = gauss_noise[:, :, 0::2]
    swapped = even_cols.reshape(2, D // 2, 2, VOCAB // 2)[:, :, ::-1, :].reshape(2, D, VOCAB // 2)
    flipper = jnp.where(jnp.arange(D) % 2 == 0, 1.0, -1.0)[None, :, None]
    odd_cols = jnp.where(pair_mark[:, None, :] > 0, swapped * flipper, gauss_noise[:, :, 1::2])
    joined = jnp.stack([even_cols, odd_cols], axis=3).reshape(2, D, VOCAB)
    pair_scale = jnp.repeat(pair_mark, 2, axis=1)[:, None, :]
    scales = jnp.where(pair_scale > 0, 1.0, scales)
    weight = jnp.clip(joined * scales / math.sqrt(D), -1.0, 1.0)
    return weight


def draw_head_weight(key, part):
    weight = head_parts(key)
    return weight.astype(jnp.bfloat16)


def draw_hidden_states(key, part):
    key = jax.random.fold_in(key, 11)
    key_state, key_scale = jax.random.split(key)
    states = jax.random.truncated_normal(key_state, -6.0, 6.0, (2, TOKENS, D), jnp.float32)
    row_scale = jnp.exp(jax.random.uniform(key_scale, (2, TOKENS, 1), jnp.float32, math.log(0.5), math.log(4.0)))
    states = states * row_scale
    return states.astype(jnp.bfloat16)


def place_ends(entries, own_key, least, top_value):
    longest = entries.shape.index(max(entries.shape))
    spots = []
    for shift in (0, 1):
        where = [jax.random.randint(jax.random.fold_in(own_key, axis), (), 0, length) for axis, length in enumerate(entries.shape)]
        where[longest] = (where[longest] + shift) % entries.shape[longest]
        spots.append(tuple(where))
    return entries.at[spots[0]].set(least).at[spots[1]].set(top_value)


def setup_inputs(seed: int = 0) -> dict:
    seeds = jax.random.split(jax.random.key(seed), 5)
    return {
        "hidden_states": draw_hidden_states(jax.random.fold_in(seeds[4], 71), 0),
        "head_weight": draw_head_weight(jax.random.fold_in(seeds[4], 71), 0),
        "targets": place_ends(jax.random.randint(seeds[2], (TOKENS,), 0, VOCAB), jax.random.fold_in(seeds[2], 1), 0, VOCAB - 1).astype(jnp.int32),
        "train_step": jax.random.randint(seeds[3], (1,), 0, WARMUP).astype(jnp.int32),
    }


def log_normalizer(values):
    peak = jnp.max(values, axis=-1, keepdims=True)
    return peak + jnp.log(jnp.sum(jnp.exp(values - peak), axis=-1, keepdims=True))


def reference(hidden_states, head_weight, targets, train_step):
    share = 0.5 * jnp.minimum(train_step[0].astype(jnp.float32) / WARMUP, 1.0)
    logits = [jnp.dot(hidden_states[index], head_weight[index], preferred_element_type=jnp.float32) for index in range(2)]
    probs = [jnp.exp(values - log_normalizer(values)) for values in logits]
    onehot = (lax.iota(jnp.int32, VOCAB)[None, :] == targets[:, None]).astype(jnp.float32)
    grad_hidden = []
    grad_head = []
    for index in range(2):
        logit_grad = ((1.0 + share) * probs[index] - onehot - share * probs[1 - index]).astype(jnp.bfloat16)
        grad_hidden.append(lax.dot_general(logit_grad, head_weight[index], (((1,), (1,)), ((), ())), preferred_element_type=jnp.float32))
        grad_head.append(lax.dot_general(hidden_states[index], logit_grad, (((0,), (0,)), ((), ())), preferred_element_type=jnp.float32))
    return jnp.stack(grad_hidden), jnp.stack(grad_head)
```

```python
import jax
import jax.numpy as jnp
from jax import lax
from jax.sharding import PartitionSpec as P

WARMUP = 1000
Z, X = 8, 4
F16 = jnp.float16
F32 = jnp.float32
BF16 = jnp.bfloat16
PROB_SCALE = 2.0**15
GRAD_SCALE = 2.0**14


def z_shift(value, k):
    return lax.ppermute(
        value, "dp", [(z * X + x, ((z + k) % Z) * X + x) for z in range(Z) for x in range(X)]
    )


def x_shift(value, k):
    return lax.ppermute(
        value, "dp", [(z * X + x, z * X + (x + k) % X) for z in range(Z) for x in range(X)]
    )


def split_shift(value, axis):
    pairs = []
    for z in range(Z):
        for x in range(X):
            for v in range(4):
                k = 1 if v % 2 == 0 else -1
                to = ((z + k) % Z) * X + x if axis == "z" else z * X + (x + k) % X
                pairs.append(((z * X + x) * 4 + v, to * 4 + v))
    return lax.ppermute(value, ("dp", "vocab"), pairs)


def vocab_flip(value, mask):
    return lax.ppermute(value, "vocab", [(v, v ^ mask) for v in range(4)])


def partner(value):
    return lax.ppermute(value, "mp", [(0, 1), (1, 0)])


def partner_z_shift(value, k):
    pairs = [
        (m * Z * X + z * X + x, (1 - m) * Z * X + ((z + k) % Z) * X + x)
        for m in range(2)
        for z in range(Z)
        for x in range(X)
    ]
    return lax.ppermute(value, ("mp", "dp"), pairs)


def combine(a, b):
    peak = jnp.maximum(a[0], b[0])
    return jnp.stack([peak, a[1] * jnp.exp(a[0] - peak) + b[1] * jnp.exp(b[0] - peak)])


def gather_blocks(hidden, core):
    mine = lax.dynamic_slice_in_dim(hidden, core * 16, 16, 0)
    from_low = x_shift(mine, 1)
    from_high = x_shift(mine, -1)
    far = split_shift(jnp.where(core == 0, from_low, from_high), "x")
    block = jnp.concatenate([mine, from_high, far, from_low], 0)
    steps = [block]
    low = high = block
    for _ in range(1, Z // 2):
        low, high = z_shift(low, 1), z_shift(high, -1)
        steps.append(jnp.concatenate([high, low], 0))
    steps.append(split_shift(jnp.where(core == 0, low, high), "z"))
    return steps


def step_rows(own, other, s):
    offsets = (s,) if s in (0, Z // 2) else (s, Z - s)
    return jnp.concatenate([own[k] for k in offsets] + [other[k] for k in offsets])


def frames(per_step):
    own, other = [None] * Z, [None] * Z
    for s, rows in enumerate(per_step):
        offsets = (s,) if s in (0, Z // 2) else (s, Z - s)
        parts = rows.reshape(2, len(offsets), 64)
        for i, k in enumerate(offsets):
            own[k], other[k] = parts[0, i], parts[1, i]
    return jnp.stack([jnp.stack(own), jnp.stack(other)])


def per_device(hidden_states, head_weight, targets, train_step):
    hidden = hidden_states[0]
    weight = head_weight[0]
    columns = weight.shape[1]
    vocab = lax.axis_index("vocab")
    dp = lax.axis_index("dp")
    core = vocab % 2
    offset = (dp * 4 + vocab) * columns
    share = 0.5 * jnp.minimum(train_step[0].astype(F32) / WARMUP, 1.0)

    fetched = gather_blocks(hidden, core)
    steps = [jnp.concatenate([rows, vocab_flip(rows, 1)], 0) for rows in fetched]
    peaks, sums, exps, partner_exps = [], [], [], []
    for rows in steps:
        logits = jnp.dot(rows, weight, preferred_element_type=F32)
        peak = jnp.max(logits, axis=-1)
        exp = jnp.exp(logits - peak[:, None])
        peaks.append(peak)
        sums.append(jnp.sum(exp, axis=-1))
        exps.append(exp)
        partner_exps.append(partner((exp * PROB_SCALE).astype(F16)))

    local_peak = frames(peaks)
    stat = jnp.stack([local_peak, frames(sums)])
    partner_peak = partner(local_peak)
    stat = combine(stat, vocab_flip(stat, 1)[:, ::-1])
    stat = combine(stat, vocab_flip(stat, 2))
    for k in (1, 2):
        stat = combine(stat, jnp.roll(x_shift(stat, -k), 16 * k, axis=3))
    for k in (1, 2):
        stat = combine(stat, jnp.roll(z_shift(stat, -k), k, axis=2))
    partner_stat = combine(partner(stat), jnp.roll(partner_z_shift(stat, -4), 4, axis=2))
    stat = combine(stat, jnp.roll(z_shift(stat, -4), 4, axis=2))
    own_factor = (1.0 + share) * jnp.exp(local_peak - stat[0]) / stat[1]
    partner_factor = (share / PROB_SCALE) * jnp.exp(partner_peak - partner_stat[0]) / partner_stat[1]

    ids = (targets - offset).reshape(Z, X, 2, 16)
    ids = lax.dynamic_slice_in_dim(jnp.concatenate([ids, ids], 0), dp // X, Z, 0)
    ids = lax.dynamic_slice_in_dim(jnp.concatenate([ids, ids], 1), dp % X, X, 1)
    ids = jnp.stack([jnp.where(core == 0, ids[:, :, 0], ids[:, :, 1]), jnp.where(core == 0, ids[:, :, 1], ids[:, :, 0])])
    ids = ids.reshape(2, Z, X * 16)

    grads = []
    for s in range(len(steps)):
        onehot = lax.iota(jnp.int32, columns)[None, :] == step_rows(ids[0], ids[1], s)[:, None]
        own = exps[s] * step_rows(own_factor[0], own_factor[1], s)[:, None]
        other = partner_exps[s].astype(F32) * step_rows(partner_factor[0], partner_factor[1], s)[:, None]
        grads.append((own - onehot.astype(F32) - other).astype(BF16))

    halves = weight.reshape(2, 2, 1024, columns)
    weight_own = lax.dynamic_index_in_dim(halves, core, 1, keepdims=False).reshape(2048, columns)
    weight_other = lax.dynamic_index_in_dim(halves, 1 - core, 1, keepdims=False).reshape(2048, columns)

    def against(grad, half):
        return GRAD_SCALE * lax.dot_general(
            grad, half, (((1,), (1,)), ((), ())), preferred_element_type=F32
        )

    blocks = [None] * Z
    for s in (4, 3, 2, 1, 0):
        grad = grads[s]
        n = grad.shape[0] // 2
        away = against(grad, weight_other).astype(F16)
        came = vocab_flip(away, 1).astype(F32)
        came = jnp.concatenate([came[n:], came[:n]], 0)
        total = against(grad, weight_own) + came
        if n == 64:
            blocks[s] = total
        else:
            blocks[s] = jnp.concatenate([total[:64], total[128:192]], 0)
            blocks[Z - s] = jnp.concatenate([total[64:128], total[192:]], 0)

    half = Z // 2
    came = split_shift(blocks[half].astype(F16), "z").astype(F32)
    up = blocks[half - 1] + jnp.where(core == 0, came, 0.0)
    down = blocks[half + 1] + jnp.where(core == 1, came, 0.0)
    for k in range(half - 1, 0, -1):
        up = z_shift(up.astype(F16), 1).astype(F32)
        down = z_shift(down.astype(F16), -1).astype(F32)
        if k > 1:
            up, down = up + blocks[k - 1], down + blocks[Z - k + 1]
    total = (blocks[0] + up + down).reshape(2, X, 16, 2048)

    came = split_shift(total[:, 2].astype(F16), "x").astype(F32)
    up = x_shift((total[:, 1] + jnp.where(core == 0, came, 0.0)).astype(F16), 1).astype(F32)
    down = x_shift((total[:, 3] + jnp.where(core == 1, came, 0.0)).astype(F16), -1).astype(F32)
    total = total[:, 0] + up + down
    total = jnp.where(core == 0, total, total[::-1]).reshape(32, 2048)
    low, high = total[:, :1024], total[:, 1024:]
    mine = jnp.where(vocab < 2, low, high)
    grad_hidden = (mine + vocab_flip(jnp.where(vocab < 2, high, low), 2)) * (1.0 / GRAD_SCALE)

    grad_head = lax.dot_general(
        jnp.concatenate(steps, 0),
        jnp.concatenate(grads, 0),
        (((0,), (0,)), ((), ())),
        preferred_element_type=F32,
    )
    return (grad_hidden[None], grad_head[None])


def solution(mesh):
    placed = (P("mp", "dp", None), P("mp", None, ("dp", "vocab")), P(), P())
    return jax.shard_map(
        per_device,
        mesh=mesh,
        in_specs=placed,
        out_specs=(P("mp", "dp", "vocab"), P("mp", None, ("dp", "vocab"))),
        check_vma=False,
    )
```

```python
import jax
import jax.numpy as jnp
import numpy as np
from jax import lax
from jax.experimental import pallas as pl
from jax.experimental.pallas import tpu as pltpu
from jax.sharding import PartitionSpec as P

WARMUP = 1000
Z, X = 8, 4
F16 = jnp.float16
F32 = jnp.float32
BF16 = jnp.bfloat16
PROB_SCALE = 2.0**15
GRAD_SCALE = 2.0**14
BIG = 384


def row_tables():
    near, wide = (0, -1, -2, 1), (-3, -4, 2, 3)
    along_z = (0, -1, 1, -2, 2, -3, 3, -4)
    along_x = ((near, 0), (near, -1), (near, 1), (near, -2), (wide, 1), (wide, -1), (wide, 2), (wide, 0))
    table = np.zeros((2, Z * X, 32), np.int32)
    for z in range(Z):
        for x in range(X):
            for i in range(8):
                for j in range(4):
                    at = i * 4 + j
                    table[0, z * X + x, at] = (z + along_z[i]) % Z * X + (x + near[j]) % X
                    offsets, shift = along_x[i]
                    table[1, z * X + x, at] = (z + offsets[j]) % Z * X + (x + shift) % X
    return table, np.argsort(table, axis=-1).astype(np.int32)


def ring(value, axes, step, cores=(0, 1)):
    pairs = []
    for z in range(Z):
        for x in range(X):
            for v in range(4):
                if v % 2 in cores:
                    if axes[v % 2] == "z":
                        to = (z + step) % Z * X + x
                    else:
                        to = z * X + (x + step) % X
                    pairs.append(((z * X + x) * 4 + v, to * 4 + v))
    return lax.ppermute(value, ("dp", "vocab"), pairs)


SMALL, LARGE = ("x", "z"), ("z", "x")


def dp_flip(value, mask):
    return lax.ppermute(value, "dp", [(i, i ^ mask) for i in range(Z * X)])


def vocab_flip(value, mask):
    return lax.ppermute(value, "vocab", [(v, v ^ mask) for v in range(4)])


def partner(value):
    return lax.ppermute(value, "mp", [(0, 1), (1, 0)])


def partner_dp_flip(value, mask):
    n = Z * X
    return lax.ppermute(
        value, ("mp", "dp"), [(m * n + i, (1 - m) * n + (i ^ mask)) for m in range(2) for i in range(n)]
    )


def reordered(table, ref):
    piece = lax.broadcasted_iota(jnp.int32, (1, 128), 1) >> 4
    rows = []
    for r in range(4):
        row = jnp.zeros((1, 128), ref.dtype)
        for c in range(8):
            at = table[r * 8 + c]
            value = pltpu.roll(ref[pl.ds(at >> 3, 1), :], ((c - (at & 7)) & 7) * 16, 1)
            row = jnp.where(piece == c, value, row)
        rows.append(row)
    return rows


def reorder_kernel(table, *refs):
    n = len(refs) // 2
    for source, out in zip(refs[:n], refs[n:]):
        for r, row in enumerate(reordered(table, source)):
            out[r : r + 1, :] = row


def reorder(table, *values):
    smem, vmem = pl.BlockSpec(memory_space=pltpu.SMEM), pl.BlockSpec(memory_space=pltpu.VMEM)
    return pl.pallas_call(
        reorder_kernel,
        in_specs=[smem] + [vmem] * len(values),
        out_shape=tuple(jax.ShapeDtypeStruct((4, 128), v.dtype) for v in values),
    )(table, *values)


def merged(*stats):
    peak = stats[0][0]
    for stat in stats[1:]:
        peak = jnp.maximum(peak, stat[0])
    return peak, sum(stat[1] * jnp.exp(stat[0] - peak) for stat in stats)


def combine(*stats):
    return jnp.stack(merged(*stats))


def factor_kernel(table, share_ref, stat, came, local, p_stat, p_came, own_ref, partner_ref, held):
    share = share_ref[0]
    for out, weight, a, b, peak in (
        (own_ref, 1.0 + share, stat, came, local[...]),
        (partner_ref, share * (1.0 / PROB_SCALE), p_stat, p_came, p_stat[2]),
    ):
        top, total = merged((a[0], a[1]), (b[0], b[1]))
        held[...] = weight * (jnp.exp(peak - top) / total)
        for r, row in enumerate(reordered(table, held)):
            out[r : r + 1, :] = row


def factors(table, share, *stats):
    smem, vmem = pl.BlockSpec(memory_space=pltpu.SMEM), pl.BlockSpec(memory_space=pltpu.VMEM)
    shape = jax.ShapeDtypeStruct((4, 128), F32)
    return pl.pallas_call(
        factor_kernel,
        in_specs=[smem, smem] + [vmem] * 5,
        out_shape=(shape, shape),
        scratch_shapes=[pltpu.VMEM((4, 128), F32)],
    )(table, share.reshape(1), *stats)


def product_kernel(own, other, weight, weight_other, out):
    dims = (((1,), (1,)), ((), ()))
    total = lax.dot_general(own[...], weight[...], dims, preferred_element_type=F32)
    total += lax.dot_general(other[...], weight_other[...], dims, preferred_element_type=F32)
    out[...] = total * GRAD_SCALE


def product(grad, weights, tile=512):
    rows, columns = grad[0].shape
    features = weights[0].shape[0]
    whole = pl.BlockSpec((rows, columns), lambda i: (0, 0))
    part = pl.BlockSpec((tile, columns), lambda i: (i, 0))
    return pl.pallas_call(
        product_kernel,
        grid=(features // tile,),
        in_specs=[whole, whole, part, part],
        out_specs=pl.BlockSpec((rows, tile), lambda i: (0, i)),
        out_shape=jax.ShapeDtypeStruct((rows, features), F32),
        compiler_params=pltpu.CompilerParams(vmem_limit_bytes=32 * 2**20),
        cost_estimate=pl.CostEstimate(
            flops=4 * rows * columns * features,
            bytes_accessed=4 * columns * features + 4 * rows * (features + columns),
            transcendentals=0,
        ),
    )(*grad, *weights)


def head_kernel(*refs):
    out = refs[-1]
    n = len(refs) // 2
    total = None
    for rows, grad in zip(refs[:n], refs[n:-1]):
        part = lax.dot_general(
            rows[...], grad[...], (((0,), (0,)), ((), ())), preferred_element_type=F32
        )
        total = part if total is None else total + part
    out[...] = total


def head(rows, grads, tile=512):
    features, columns = rows[0].shape[1], grads[0].shape[1]
    return pl.pallas_call(
        head_kernel,
        grid=(features // tile,),
        in_specs=[pl.BlockSpec((r.shape[0], tile), lambda i: (0, i)) for r in rows]
        + [pl.BlockSpec(g.shape, lambda i: (0, 0)) for g in grads],
        out_specs=pl.BlockSpec((tile, columns), lambda i: (i, 0)),
        out_shape=jax.ShapeDtypeStruct((features, columns), F32),
        compiler_params=pltpu.CompilerParams(vmem_limit_bytes=32 * 2**20),
        cost_estimate=pl.CostEstimate(
            flops=4 * 1024 * columns * features // 2,
            bytes_accessed=2048 * features + 4 * columns * features,
            transcendentals=0,
        ),
    )(*rows, *grads)


def per_device(hidden_states, head_weight, targets, train_step):
    hidden = hidden_states[0]
    weight = head_weight[0]
    columns = weight.shape[1]
    vocab = lax.axis_index("vocab")
    dp = lax.axis_index("dp")
    core = vocab % 2
    share = 0.5 * jnp.minimum(train_step[0].astype(F32) / WARMUP, 1.0)
    to_local, to_global = (
        lax.dynamic_index_in_dim(jnp.asarray(t.reshape(64, 32)), core * 32 + dp, 0, keepdims=False)
        for t in row_tables()
    )

    mine = lax.dynamic_slice_in_dim(hidden, core * 16, 16, 0)
    u1, d1 = ring(mine, SMALL, 1), ring(mine, SMALL, -1)
    u2, d2 = ring(u1, SMALL, 1), ring(d1, SMALL, -1, (1,))
    near = jnp.concatenate([mine, u1, u2, d1], 0)
    up1, down1 = ring(near, LARGE, 1), ring(near, LARGE, -1)
    u3, d3 = ring(u2, SMALL, 1, (1,)), ring(d2, SMALL, -1, (1,))
    u4 = ring(u3, SMALL, 1, (1,))
    wide = jnp.concatenate([u3, u4, d2, d3], 0)
    up2 = ring(up1, LARGE, 1)
    down2 = ring(jnp.where(core == 0, down1, wide), LARGE, -1)
    up3 = ring(jnp.where(core == 0, up2, wide), LARGE, 1)
    down3 = ring(down2, LARGE, -1)

    weights = (weight, vocab_flip(weight, 1))
    ids = lax.dynamic_index_in_dim(targets.reshape(32, 2, 16), core, 1, keepdims=False)
    (ids,) = reorder(to_local, ids.reshape(4, 128))
    ids = ids.reshape(512)

    def scores(rows):
        logits = [jnp.dot(rows, w, preferred_element_type=F32) for w in weights]
        peak = jnp.maximum(*[jnp.max(part, axis=-1) for part in logits])
        exps = [jnp.exp(part - peak[:, None]) for part in logits]
        total = jnp.sum(exps[0], axis=-1) + jnp.sum(exps[1], axis=-1)
        sent = partner(jnp.concatenate([(e * PROB_SCALE).astype(F16) for e in exps], 1))
        return peak, total, exps, sent

    rows = [jnp.concatenate([near, up1, down1, up2, down2, up3], 0)]
    results = [scores(rows[0])]
    far = ring(up3, LARGE, 1, (0,))
    rows.append(jnp.concatenate([down3, jnp.where(core == 0, far, wide)], 0))
    results.append(scores(rows[1]))

    peak, total = reorder(
        to_global, *[jnp.concatenate([r[i] for r in results]).reshape(4, 128) for i in range(2)]
    )
    stat = jnp.stack([peak, total])
    stat = combine(stat, *[dp_flip(stat, k) for k in (1, 2, 3)])
    stat = combine(stat, *[dp_flip(stat, 4 * k) for k in (1, 2, 3)])
    stat = combine(stat, vocab_flip(stat, 2))
    own_factor, partner_factor = factors(
        to_local,
        share,
        stat,
        dp_flip(stat, 16),
        peak,
        partner(jnp.concatenate([stat, peak[None]], 0)),
        partner_dp_flip(stat, 16),
    )
    own_factor, partner_factor = own_factor.reshape(512), partner_factor.reshape(512)

    grads = []
    for part, (_, _, exps, sent) in zip((slice(0, BIG), slice(BIG, 512)), results):
        sides = []
        for side in range(2):
            first = (dp * 4 + (vocab ^ side)) * columns
            onehot = (first + lax.iota(jnp.int32, columns))[None, :] == ids[part][:, None]
            other = sent[:, side * columns : (side + 1) * columns].astype(F32)
            grad = exps[side] * own_factor[part][:, None] - onehot.astype(F32)
            sides.append((grad - other * partner_factor[part][:, None]).astype(BF16))
        grads.append(sides)

    last = product(grads[1], weights)
    p_down3, p_far = last[:64], last[64:]
    sent_far, held = lax.optimization_barrier((p_far.astype(F16), grads[0]))
    first = product(held, weights)
    p_near, p_up1, p_down1, p_up2, p_down2, p_up3 = (first[64 * i : 64 * i + 64] for i in range(6))

    def pass_on(value, axes, step, cores=(0, 1)):
        return ring(value.astype(F16), axes, step, cores).astype(F32)

    def only(which, value):
        return jnp.where(core == which, value, 0.0)

    c1 = ring(sent_far, LARGE, -1, (0,)).astype(F32)
    c2d = pass_on(p_down3, LARGE, 1)
    c2u = pass_on(p_up3 + c1, LARGE, -1)
    c3d = pass_on(p_down2 + c2d, LARGE, 1)
    c3u = pass_on(p_up2 + only(0, c2u), LARGE, -1)
    c4d = pass_on(p_down1 + only(0, c3d), LARGE, 1)
    c4u = pass_on(p_up1 + c3u, LARGE, -1)
    p_wide = (p_far + c2u + c3d).reshape(4, 16, 4096)
    e1 = pass_on(p_wide[1], SMALL, -1, (1,))
    e2d = pass_on(p_wide[3], SMALL, 1, (1,))
    e2u = pass_on(p_wide[0] + e1, SMALL, -1, (1,))
    e3d = pass_on(p_wide[2] + e2d, SMALL, 1, (1,))
    p_near = (p_near + c4u + c4d).reshape(4, 16, 4096)
    e3u = pass_on(p_near[2] + e2u, SMALL, -1)
    e4d = pass_on(p_near[3] + e3d, SMALL, 1)
    e4u = pass_on(p_near[1] + e3u, SMALL, -1)
    total = p_near[0] + e4u + e4d

    low, high = total[:, :2048], total[:, 2048:]
    came = vocab_flip(jnp.where(vocab < 2, high, low).astype(F16), 2).astype(F32)
    total = jnp.where(vocab < 2, low, high) + came
    low, high = total[:, :1024], total[:, 1024:]
    came = vocab_flip(jnp.where(core == 0, high, low), 1)
    grad_hidden = jnp.concatenate(
        [jnp.where(core == 0, low, came), jnp.where(core == 0, came, high)], 0
    ) * (1.0 / GRAD_SCALE)

    grad_head = head(
        rows + [vocab_flip(r, 1) for r in rows],
        [g[0] for g in grads] + [vocab_flip(g[1], 1) for g in grads],
    )
    return (grad_hidden[None], grad_head[None])


def solution(mesh):
    placed = (P("mp", "dp", None), P("mp", None, ("dp", "vocab")), P(), P())
    return jax.shard_map(
        per_device,
        mesh=mesh,
        in_specs=placed,
        out_specs=(P("mp", "dp", "vocab"), P("mp", None, ("dp", "vocab"))),
        check_vma=False,
    )
```

```python
import jax
import jax.numpy as jnp
import numpy as np
from jax import lax
from jax.experimental import pallas as pl
from jax.experimental.pallas import tpu as pltpu
from jax.sharding import PartitionSpec as P

WARMUP = 1000
Z, X = 8, 4
F16 = jnp.float16
F32 = jnp.float32
BF16 = jnp.bfloat16
PROB_SCALE = 2.0**15
GRAD_SCALE = 2.0**14


def row_tables():
    near, wide = (0, -1, -2, 1), (-3, -4, 2, 3)
    along_z = (0, -1, 1, -2, 2, -3, 3, -4)
    along_x = ((near, 0), (near, -1), (near, 1), (near, -2), (wide, 0), (wide, -1), (wide, 1), (wide, -2))
    table = np.zeros((2, Z * X, 32), np.int32)
    for z in range(Z):
        for x in range(X):
            for i in range(8):
                for j in range(4):
                    at = i * 4 + j
                    table[0, z * X + x, at] = (z + along_z[i]) % Z * X + (x + near[j]) % X
                    offsets, shift = along_x[i]
                    table[1, z * X + x, at] = (z + offsets[j]) % Z * X + (x + shift) % X
    return table, np.argsort(table, axis=-1).astype(np.int32)


def ring(value, axes, step, cores=(0, 1)):
    pairs = []
    for z in range(Z):
        for x in range(X):
            for v in range(4):
                if v % 2 in cores:
                    if axes[v % 2] == "z":
                        to = (z + step) % Z * X + x
                    else:
                        to = z * X + (x + step) % X
                    pairs.append(((z * X + x) * 4 + v, to * 4 + v))
    return lax.ppermute(value, ("dp", "vocab"), pairs)


SMALL, LARGE = ("x", "z"), ("z", "x")


def dp_flip(value, mask):
    return lax.ppermute(value, "dp", [(i, i ^ mask) for i in range(Z * X)])


def vocab_flip(value, mask):
    return lax.ppermute(value, "vocab", [(v, v ^ mask) for v in range(4)])


def partner(value):
    return lax.ppermute(value, "mp", [(0, 1), (1, 0)])


def partner_vocab_flip(value, mask):
    pairs = [
        ((m * Z * X + i) * 4 + v, ((1 - m) * Z * X + i) * 4 + (v ^ mask))
        for m in range(2)
        for i in range(Z * X)
        for v in range(4)
    ]
    return lax.ppermute(value, ("mp", "dp", "vocab"), pairs)


def reordered(place, ref):
    piece = lax.broadcasted_iota(jnp.int32, (1, 128), 1) >> 4
    rows = []
    for r in range(4):
        row = jnp.zeros((1, 128), ref.dtype)
        for c in range(8):
            at = place(r * 8 + c)
            value = pltpu.roll(ref[pl.ds(at >> 3, 1), :], ((c - (at & 7)) & 7) * 16, 1)
            row = jnp.where(piece == c, value, row)
        rows.append(row)
    return rows


def ids_kernel(table, core, source, out):
    for r, row in enumerate(reordered(lambda p: 2 * table[p] + core[0], source)):
        out[r : r + 1, :] = row


def local_ids(table, core, targets):
    smem, vmem = pl.BlockSpec(memory_space=pltpu.SMEM), pl.BlockSpec(memory_space=pltpu.VMEM)
    return pl.pallas_call(
        ids_kernel,
        in_specs=[smem, smem, vmem],
        out_shape=jax.ShapeDtypeStruct((4, 128), jnp.int32),
    )(table, core.reshape(1), targets.reshape(8, 128))


def stat_kernel(table, *refs):
    out, held = refs[-2:]
    for which in range(2):
        for g in range(4):
            held[g : g + 1, :] = refs[which * 4 + g][...]
        for r, row in enumerate(reordered(lambda p: table[32 + p], held)):
            out[which, r : r + 1, :] = row


def statistics(table, peaks, sums):
    smem, vmem = pl.BlockSpec(memory_space=pltpu.SMEM), pl.BlockSpec(memory_space=pltpu.VMEM)
    return pl.pallas_call(
        stat_kernel,
        in_specs=[smem] + [vmem] * 8,
        out_shape=jax.ShapeDtypeStruct((2, 4, 128), F32),
        scratch_shapes=[pltpu.VMEM((4, 128), F32)],
    )(table, *peaks, *sums)


def merged(*stats):
    peak = stats[0][0]
    for stat in stats[1:]:
        peak = jnp.maximum(peak, stat[0])
    return peak, sum(stat[1] * jnp.exp(stat[0] - peak) for stat in stats)


def combine(*stats):
    return jnp.stack([*merged(*[s[:2] for s in stats]), *merged(*[s[2:] for s in stats])])


def factor_kernel(table, share_ref, stat, came, own_peak, partner_peak, *refs):
    share = share_ref[0]
    held = refs[-1]
    for which, weight, peak in (
        (0, 1.0 + share, own_peak),
        (1, share * (1.0 / PROB_SCALE), partner_peak),
    ):
        first = 2 * which
        top, total = merged((stat[first], stat[first + 1]), (came[first], came[first + 1]))
        held[...] = weight * (jnp.exp(peak[...] - top) / total)
        for r, row in enumerate(reordered(lambda p: table[p], held)):
            refs[which * 4 + r][...] = row


def factors(table, share, *stats):
    smem, vmem = pl.BlockSpec(memory_space=pltpu.SMEM), pl.BlockSpec(memory_space=pltpu.VMEM)
    out = pl.pallas_call(
        factor_kernel,
        in_specs=[smem, smem] + [vmem] * 4,
        out_shape=(jax.ShapeDtypeStruct((1, 128), F32),) * 8,
        scratch_shapes=[pltpu.VMEM((4, 128), F32)],
    )(table, share.reshape(1), *stats)
    out = [v.reshape(128) for v in out]
    return out[:4], out[4:]


def score_kernel(a, b, own, other, exps, peaks, sums, logits):
    k = pl.program_id(0)
    rows = jnp.concatenate([a[...], b[...]], 0)
    columns = own.shape[1]
    for side, weight in enumerate((own, other)):
        part = jnp.dot(rows, weight[...], preferred_element_type=F32)
        at = pl.ds(side * columns, columns)

        @pl.when(k == 0)
        def _():
            logits[:, at] = part

        @pl.when(k > 0)
        def _():
            logits[:, at] += part

    @pl.when(k == pl.num_programs(0) - 1)
    def _():
        peak = jnp.max(logits[...], axis=1, keepdims=True)
        value = jnp.exp(logits[...] - peak)
        exps[...] = value
        total = jnp.sum(value, axis=1, keepdims=True)
        peaks[...] = jnp.broadcast_to(peak, (128, 128)).T[:1]
        sums[...] = jnp.broadcast_to(total, (128, 128)).T[:1]


def score(a, b, own, other, tile=1024):
    features, columns = own.shape
    rows = pl.BlockSpec((64, tile), lambda k: (0, k))
    weight = pl.BlockSpec((tile, columns), lambda k: (k, 0))
    line = jax.ShapeDtypeStruct((1, 128), F32)
    line_spec = pl.BlockSpec((1, 128), lambda k: (0, 0))
    return pl.pallas_call(
        score_kernel,
        grid=(features // tile,),
        in_specs=[rows, rows, weight, weight],
        out_specs=(pl.BlockSpec((128, 2 * columns), lambda k: (0, 0)), line_spec, line_spec),
        out_shape=(jax.ShapeDtypeStruct((128, 2 * columns), F32), line, line),
        scratch_shapes=[pltpu.VMEM((128, 2 * columns), F32)],
        compiler_params=pltpu.CompilerParams(vmem_limit_bytes=12 * 2**20),
        cost_estimate=pl.CostEstimate(flops=1000, bytes_accessed=1000, transcendentals=0),
    )(a, b, own, other)


def head_kernel(n, *refs):
    out, held = refs[-2:]

    @pl.when(pl.program_id(0) == 0)
    def _():
        at = 0
        for grad in refs[n:-2]:
            held[at : at + grad.shape[0], :] = grad[...]
            at += grad.shape[0]

    rows = jnp.concatenate([r[...] for r in refs[:n]], 0)
    out[...] = lax.dot_general(
        rows, held[...], (((0,), (0,)), ((), ())), preferred_element_type=F32
    )


def head(rows, grads, columns, tile=512):
    features = rows[0].shape[1]
    total = sum(r.shape[0] for r in rows)
    return pl.pallas_call(
        lambda *refs: head_kernel(len(rows), *refs),
        grid=(features // tile,),
        in_specs=[pl.BlockSpec((r.shape[0], tile), lambda i: (0, i)) for r in rows]
        + [pl.BlockSpec((g.shape[0], columns), lambda i: (0, 0)) for g in grads],
        out_specs=pl.BlockSpec((tile, columns), lambda i: (i, 0)),
        out_shape=jax.ShapeDtypeStruct((features, columns), F32),
        scratch_shapes=[pltpu.VMEM((total, columns), BF16)],
        compiler_params=pltpu.CompilerParams(vmem_limit_bytes=50 * 2**20),
        cost_estimate=pl.CostEstimate(
            flops=2 * total * columns * features,
            bytes_accessed=2 * total * features + 4 * columns * features,
            transcendentals=0,
        ),
    )(*rows, *grads)


def after(value, *earlier):
    return lax.optimization_barrier((value, *earlier))[0]


def together(*values):
    return lax.optimization_barrier(values)


def per_device(hidden_states, head_weight, targets, train_step):
    hidden = hidden_states[0]
    weight = head_weight[0]
    columns = weight.shape[1]
    vocab = lax.axis_index("vocab")
    dp = lax.axis_index("dp")
    core = vocab % 2
    share = 0.5 * jnp.minimum(train_step[0].astype(F32) / WARMUP, 1.0)
    mine = lax.dynamic_slice_in_dim(hidden, core * 16, 16, 0)
    weight_other = vocab_flip(weight, 1)
    u1, d1, u2 = together(ring(mine, SMALL, 1), ring(mine, SMALL, -1), ring(mine, SMALL, 2))
    near = jnp.concatenate([mine, u1, u2, d1], 0)
    up1, down1 = ring(near, LARGE, 1), ring(near, LARGE, -1)
    targets, place, d1 = after((targets, core * 32 + dp, d1), near)
    table = jnp.asarray(np.concatenate([t.reshape(64, 32) for t in row_tables()], 1))
    table = lax.dynamic_index_in_dim(table, place, 0, keepdims=False)
    ids = local_ids(table, core, targets)
    u3, d2 = together(ring(u2, SMALL, 1, (1,)), ring(d1, SMALL, -1, (1,)))
    up1, down1, u3, d2, weight_other, ids, table = together(
        up1, down1, u3, d2, weight_other, ids, table
    )

    both = jnp.concatenate([weight, weight_other], 1)
    column_ids = jnp.concatenate(
        [(dp * 4 + v) * columns + lax.iota(jnp.int32, columns) for v in (vocab, vocab ^ 1)]
    )

    def scores(a, b):
        exps, peak, total = score(a, b, weight, weight_other)
        return exps, (exps * PROB_SCALE).astype(F16), peak, total

    def flip(*blocks):
        return [vocab_flip(b, 1) for b in blocks]

    up2, down2 = ring(up1, LARGE, 1), ring(down1, LARGE, -1, (0,))
    u4, d3 = ring(u3, SMALL, 1, (1,)), ring(d2, SMALL, -1, (1,))
    group0 = scores(near, up1)
    up2, down2, u4, d3, exps0 = together(up2, down2, u4, d3, group0[0])
    wide = jnp.concatenate([u3, u4, d2, d3], 0)
    far2 = jnp.where(core == 0, down2, wide)
    up3 = ring(jnp.where(core == 0, up2, wide), LARGE, 1)
    down3 = ring(far2, LARGE, -1)
    group1 = scores(down1, up2)
    up3, down3, exps1, sent0 = together(up3, down3, group1[0], partner(group0[1]))
    far = ring(up3, LARGE, 1)
    group2 = scores(far2, up3)
    far, exps2, sent1 = together(far, group2[0], partner(group1[1]))
    group3 = scores(down3, far)
    rows = [near, up1, down1, up2, far2, up3, down3, far]
    exps = (exps0, exps1, exps2, group3[0])
    _, small, peaks, sums = zip(group0, group1, group2, group3)

    stat = statistics(table, peaks, sums)
    own_peak = stat[0]
    came, p_stat, p_came = together(
        vocab_flip(stat, 2), partner(stat), partner_vocab_flip(stat, 2)
    )
    partner_peak = p_stat[0]
    stat = jnp.stack([*merged(stat, came), *merged(p_stat, p_came)])
    small2, small3, turned = after((small[2], small[3], rows), stat)
    came = [dp_flip(stat, k) for k in (1, 2, 3)]
    came, other0 = together(came, flip(*turned[:2]))
    turned = after(turned, *other0)
    stat = combine(stat, *came)
    sent = (sent0, sent1, partner(small2), partner(small3))
    came, other1 = together([dp_flip(stat, 4 * k) for k in (1, 2, 3)], flip(*turned[2:4]))
    stat = combine(stat, *came)
    own_factor, partner_factor = factors(
        table, share, stat, dp_flip(stat, 16), own_peak, partner_peak
    )
    own_factor, partner_factor, sent = together(own_factor, partner_factor, sent)

    def gradient(g):
        onehot = column_ids[None, :] == ids[g][:, None]
        grad = exps[g] * own_factor[g][:, None] - onehot.astype(F32)
        return (grad - sent[g].astype(F32) * partner_factor[g][:, None]).astype(BF16)

    def product(grad):
        return GRAD_SCALE * lax.dot_general(
            grad, both, (((1,), (1,)), ((), ())), preferred_element_type=F32
        )

    def wider(value):
        return value.astype(F32)

    def only(which, value):
        return jnp.where(core == which, value.astype(F32), 0.0)

    grad3 = gradient(3)
    p_last, turned = together(product(grad3), turned)
    far = p_last[64:].astype(F16)
    c1 = ring(far, LARGE, -1)
    grad012 = after(jnp.concatenate([gradient(g) for g in range(3)], 0), far)
    p_rest = product(grad012)
    grads = [grad012, grad3]
    grads_other = [vocab_flip(g[:, columns:], 1) for g in grads]
    c1, p_rest, other2 = together(c1, p_rest, flip(*turned[4:]))
    rows_other = [*other0, *other1, *other2]
    p_near, p_up1, p_down1, p_up2, p_far2, p_up3 = (p_rest[64 * i : 64 * i + 64] for i in range(6))

    def step(up, down, cores=(0, 1)):
        up, down = together(up.astype(F16), down.astype(F16))
        return ring(up, LARGE, -1), ring(down, LARGE, 1, cores)

    def pass_on(value, step, cores=(0, 1)):
        return ring(value.astype(F16), SMALL, step, cores)

    c2u, c2d, grads_other = together(*step(p_up3 + wider(c1), p_last[:64]), grads_other)
    p_far2 = p_far2 + wider(c2d) + only(1, c2u)
    c3u, c3d = step(p_up2 + only(0, c2u), p_far2, (0,))
    p_wide = p_far2.reshape(4, 16, 4096)
    e1, e2d = pass_on(p_wide[1], -1, (1,)), pass_on(p_wide[3], 1, (1,))
    grad_head = head([*rows, *rows_other], [*grads, *grads_other], columns)
    c3u, c3d, e1, e2d, grad_head = together(c3u, c3d, e1, e2d, grad_head)
    c4u, c4d = step(p_up1 + wider(c3u), p_down1 + wider(c3d))
    e2u = pass_on(p_wide[0] + wider(e1), -1, (1,))
    e3d = pass_on(p_wide[2] + wider(e2d), 1, (1,))
    c4u, c4d, e2u, e3d = together(c4u, c4d, e2u, e3d)
    p_near = (p_near + wider(c4u) + wider(c4d)).reshape(4, 16, 4096)
    e4u, e4d, e3u = together(
        pass_on(p_near[1], -1),
        pass_on(p_near[3] + wider(e3d), 1),
        pass_on(p_near[2] + wider(e2u), -2),
    )
    total = p_near[0] + wider(e4u) + wider(e4d) + wider(e3u)

    low, high = total[:, :2048], total[:, 2048:]
    came = vocab_flip(jnp.where(vocab < 2, high, low).astype(F16), 2).astype(F32)
    total = jnp.where(vocab < 2, low, high) + came
    low, high = total[:, :1024], total[:, 1024:]
    came = vocab_flip(jnp.where(core == 0, high, low), 1)
    grad_hidden = jnp.concatenate(
        [jnp.where(core == 0, low, came), jnp.where(core == 0, came, high)], 0
    ) * (1.0 / GRAD_SCALE)
    return (grad_hidden[None], grad_head[None])


def solution(mesh):
    placed = (P("mp", "dp", None), P("mp", None, ("dp", "vocab")), P(), P())
    return jax.shard_map(
        per_device,
        mesh=mesh,
        in_specs=placed,
        out_specs=(P("mp", "dp", "vocab"), P("mp", None, ("dp", "vocab"))),
        check_vma=False,
    )
```

```python
import jax
import jax.numpy as jnp
import numpy as np
from jax import lax
from jax.experimental import pallas as pl
from jax.experimental.pallas import tpu as pltpu
from jax.sharding import PartitionSpec as P

WARMUP = 1000
Z, X = 8, 4
F16 = jnp.float16
F32 = jnp.float32
BF16 = jnp.bfloat16
PROB_SCALE = 2.0**15
GRAD_SCALE = 2.0**14


def row_tables():
    near, wide = (0, -1, -2, 1), (-3, -4, 2, 3)
    along_z = (0, -1, 1, -2, 2, -3, 3, -4)
    along_x = ((near, 0), (near, -1), (near, 1), (near, -2), (wide, 0), (wide, -1), (wide, 1), (wide, -2))
    table = np.zeros((2, Z * X, 32), np.int32)
    for z in range(Z):
        for x in range(X):
            for i in range(8):
                for j in range(4):
                    at = i * 4 + j
                    table[0, z * X + x, at] = (z + along_z[i]) % Z * X + (x + near[j]) % X
                    offsets, shift = along_x[i]
                    table[1, z * X + x, at] = (z + offsets[j]) % Z * X + (x + shift) % X
    return table, np.argsort(table, axis=-1).astype(np.int32)


def ring(value, axes, step, cores=(0, 1)):
    pairs = []
    for z in range(Z):
        for x in range(X):
            for v in range(4):
                if v % 2 in cores:
                    if axes[v % 2] == "z":
                        to = (z + step) % Z * X + x
                    else:
                        to = z * X + (x + step) % X
                    pairs.append(((z * X + x) * 4 + v, to * 4 + v))
    return lax.ppermute(value, ("dp", "vocab"), pairs)


SMALL, LARGE = ("x", "z"), ("z", "x")


def dp_flip(value, mask):
    return lax.ppermute(value, "dp", [(i, i ^ mask) for i in range(Z * X)])


def vocab_flip(value, mask):
    return lax.ppermute(value, "vocab", [(v, v ^ mask) for v in range(4)])


def partner(value):
    return lax.ppermute(value, "mp", [(0, 1), (1, 0)])


def partner_vocab_flip(value, mask):
    pairs = [
        ((m * Z * X + i) * 4 + v, ((1 - m) * Z * X + i) * 4 + (v ^ mask))
        for m in range(2)
        for i in range(Z * X)
        for v in range(4)
    ]
    return lax.ppermute(value, ("mp", "dp", "vocab"), pairs)


def reordered(place, ref):
    piece = lax.broadcasted_iota(jnp.int32, (1, 128), 1) >> 4
    rows = []
    for r in range(4):
        row = jnp.zeros((1, 128), ref.dtype)
        for c in range(8):
            at = place(r * 8 + c)
            value = pltpu.roll(ref[pl.ds(at >> 3, 1), :], ((c - (at & 7)) & 7) * 16, 1)
            row = jnp.where(piece == c, value, row)
        rows.append(row)
    return rows


def ids_kernel(table, core, source, out):
    for r, row in enumerate(reordered(lambda p: 2 * table[p] + core[0], source)):
        out[r : r + 1, :] = row


def local_ids(table, core, targets):
    smem, vmem = pl.BlockSpec(memory_space=pltpu.SMEM), pl.BlockSpec(memory_space=pltpu.VMEM)
    return pl.pallas_call(
        ids_kernel,
        in_specs=[smem, smem, vmem],
        out_shape=jax.ShapeDtypeStruct((4, 128), jnp.int32),
    )(table, core.reshape(1), targets.reshape(8, 128))


def stat_kernel(table, *refs):
    out, held = refs[-2:]
    for which in range(2):
        at = 0
        for lines in refs[:-2]:
            for i in range(lines.shape[0]):
                held[at : at + 1, :] = lines[i, which : which + 1, :]
                at += 1
        for r, row in enumerate(reordered(lambda p: table[32 + p], held)):
            out[which, r : r + 1, :] = row


def statistics(table, lines):
    smem, vmem = pl.BlockSpec(memory_space=pltpu.SMEM), pl.BlockSpec(memory_space=pltpu.VMEM)
    return pl.pallas_call(
        stat_kernel,
        in_specs=[smem] + [vmem] * len(lines),
        out_shape=jax.ShapeDtypeStruct((2, 4, 128), F32),
        scratch_shapes=[pltpu.VMEM((4, 128), F32)],
    )(table, *lines)


def merged(*stats):
    peak = stats[0][0]
    for stat in stats[1:]:
        peak = jnp.maximum(peak, stat[0])
    return peak, sum(stat[1] * jnp.exp(stat[0] - peak) for stat in stats)


def combine(*stats):
    return jnp.stack([*merged(*[s[:2] for s in stats]), *merged(*[s[2:] for s in stats])])


def factor_kernel(table, share_ref, stat, came, own_peak, partner_peak, *refs):
    share = share_ref[0]
    held = refs[-1]
    for which, weight, peak in (
        (0, 1.0 + share, own_peak),
        (1, share * (1.0 / PROB_SCALE), partner_peak),
    ):
        first = 2 * which
        top, total = merged((stat[first], stat[first + 1]), (came[first], came[first + 1]))
        held[...] = weight * (jnp.exp(peak[...] - top) / total)
        for r, row in enumerate(reordered(lambda p: table[p], held)):
            refs[which * 4 + r][...] = row


def factors(table, share, *stats):
    smem, vmem = pl.BlockSpec(memory_space=pltpu.SMEM), pl.BlockSpec(memory_space=pltpu.VMEM)
    out = pl.pallas_call(
        factor_kernel,
        in_specs=[smem, smem] + [vmem] * 4,
        out_shape=(jax.ShapeDtypeStruct((1, 128), F32),) * 8,
        scratch_shapes=[pltpu.VMEM((4, 128), F32)],
    )(table, share.reshape(1), *stats)
    out = [v.reshape(128) for v in out]
    return out[:4], out[4:]


def score_kernel(n, *refs):
    own, other, exps, lines, logits, held, done = refs[n:]
    steps, _, tile, columns = held.shape
    copies = [
        [
            pltpu.make_async_copy(w.at[pl.ds(k * tile, tile), :], held.at[k, side], done.at[k, side])
            for side, w in enumerate((own, other))
        ]
        for k in range(steps)
    ]
    for pair in copies:
        for copy in pair:
            copy.start()
    for k in range(steps):
        rows = jnp.concatenate([r[:, k * tile : (k + 1) * tile] for r in refs[:n]], 0)
        for side in range(2):
            copies[k][side].wait()
            part = jnp.dot(rows, held[k, side], preferred_element_type=F32)
            at = pl.ds(side * columns, columns)
            if k == 0:
                logits[:, at] = part
            else:
                logits[:, at] += part
    for i in range(n // 2):
        at = pl.ds(i * 128, 128)
        peak = jnp.max(logits[at, :], axis=1, keepdims=True)
        value = jnp.exp(logits[at, :] - peak)
        exps[at, :] = value
        total = jnp.sum(value, axis=1, keepdims=True)
        for which, column in enumerate((peak, total)):
            lines[i, which : which + 1, :] = jnp.broadcast_to(column, (128, 128)).T[:1]


def score(blocks, own, other, tile=1024):
    features, columns = own.shape
    n = len(blocks)
    vmem, hbm = pl.BlockSpec(memory_space=pltpu.VMEM), pl.BlockSpec(memory_space=pltpu.HBM)
    return pl.pallas_call(
        lambda *refs: score_kernel(n, *refs),
        in_specs=[vmem] * n + [hbm, hbm],
        out_specs=(vmem, vmem),
        out_shape=(
            jax.ShapeDtypeStruct((64 * n, 2 * columns), F32),
            jax.ShapeDtypeStruct((n // 2, 2, 128), F32),
        ),
        scratch_shapes=[
            pltpu.VMEM((64 * n, 2 * columns), F32),
            pltpu.VMEM((features // tile, 2, tile, columns), BF16),
            pltpu.SemaphoreType.DMA((features // tile, 2)),
        ],
        compiler_params=pltpu.CompilerParams(vmem_limit_bytes=20 * 2**20),
        cost_estimate=pl.CostEstimate(flops=1000, bytes_accessed=1000, transcendentals=0),
    )(*blocks, own, other)


def head_kernel(n, *refs):
    out, held = refs[-2:]

    @pl.when(pl.program_id(0) == 0)
    def _():
        at = 0
        for grad in refs[n:-2]:
            held[at : at + grad.shape[0], :] = grad[...]
            at += grad.shape[0]

    rows = jnp.concatenate([r[...] for r in refs[:n]], 0)
    out[...] = lax.dot_general(
        rows, held[...], (((0,), (0,)), ((), ())), preferred_element_type=F32
    )


def head(rows, grads, columns, first, steps, before=None, tile=512):
    features = rows[0].shape[1]
    total = sum(r.shape[0] for r in rows)
    earlier = [] if before is None else [before]

    def kernel(*refs):
        head_kernel(len(rows), *refs[: len(rows) + len(grads)], *refs[-2:])

    return pl.pallas_call(
        kernel,
        grid=(steps,),
        in_specs=[pl.BlockSpec((r.shape[0], tile), lambda i: (0, first + i)) for r in rows]
        + [pl.BlockSpec((g.shape[0], columns), lambda i: (0, 0)) for g in grads]
        + [pl.BlockSpec(memory_space=pl.ANY)] * len(earlier),
        out_specs=pl.BlockSpec((tile, columns), lambda i: (first + i, 0)),
        out_shape=jax.ShapeDtypeStruct((features, columns), F32),
        scratch_shapes=[pltpu.VMEM((total, columns), BF16)],
        input_output_aliases={len(rows) + len(grads): 0} if earlier else {},
        compiler_params=pltpu.CompilerParams(vmem_limit_bytes=50 * 2**20),
        cost_estimate=pl.CostEstimate(flops=1000, bytes_accessed=1000, transcendentals=0),
    )(*rows, *grads, *earlier)


def after(value, *earlier):
    return lax.optimization_barrier((value, *earlier))[0]


def together(*values):
    return lax.optimization_barrier(values)


def per_device(hidden_states, head_weight, targets, train_step):
    hidden = hidden_states[0]
    weight = head_weight[0]
    columns = weight.shape[1]
    vocab = lax.axis_index("vocab")
    dp = lax.axis_index("dp")
    core = vocab % 2
    share = 0.5 * jnp.minimum(train_step[0].astype(F32) / WARMUP, 1.0)
    mine = lax.dynamic_slice_in_dim(hidden, core * 16, 16, 0)
    weight_other = vocab_flip(weight, 1)
    u2, d1, u1 = together(ring(mine, SMALL, 2), ring(mine, SMALL, -1), ring(mine, SMALL, 1))
    near = jnp.concatenate([mine, u1, u2, d1], 0)
    up1, down1 = ring(near, LARGE, 1), ring(near, LARGE, -1)
    targets, place, d1 = after((targets, core * 32 + dp, d1), near)
    table = jnp.asarray(np.concatenate([t.reshape(64, 32) for t in row_tables()], 1))
    table = lax.dynamic_index_in_dim(table, place, 0, keepdims=False)
    ids = local_ids(table, core, targets)
    u3, d2 = together(ring(u2, SMALL, 1, (1,)), ring(d1, SMALL, -1, (1,)))
    up1, down1, u3, d2, weight_other, ids, table = together(
        up1, down1, u3, d2, weight_other, ids, table
    )

    both = jnp.concatenate([weight, weight_other], 1)
    column_ids = jnp.concatenate(
        [(dp * 4 + v) * columns + lax.iota(jnp.int32, columns) for v in (vocab, vocab ^ 1)]
    )

    def scores(*blocks):
        exps, lines = score(blocks, weight, weight_other)
        return exps, (exps * PROB_SCALE).astype(F16), lines

    def flip(*blocks):
        return [vocab_flip(b, 1) for b in blocks]

    up2, down2 = ring(up1, LARGE, 1), ring(down1, LARGE, -1, (0,))
    u4, d3 = ring(u3, SMALL, 1, (1,)), ring(d2, SMALL, -1, (1,))
    up2, down2, u4, d3, weight_other = together(up2, down2, u4, d3, weight_other)
    wide = jnp.concatenate([u3, u4, d2, d3], 0)
    far2 = jnp.where(core == 0, down2, wide)
    up3 = ring(jnp.where(core == 0, up2, wide), LARGE, 1)
    down3 = ring(far2, LARGE, -1)
    first = scores(near, up1, down1, up2)
    up3, down3, exps0 = together(up3, down3, first[0])
    far = ring(up3, LARGE, 1)
    second = scores(far2, up3)
    far, exps1, sent0 = together(far, second[0], partner(first[1]))
    third = scores(down3, far)
    lines, sent1 = after((third[2], partner(second[1])), third[0])
    rows = [near, up1, down1, up2, far2, up3, down3, far]

    stat = statistics(table, (first[2], second[2], lines))
    own_peak = stat[0]
    came, p_came, p_stat = together(
        vocab_flip(stat, 2), partner_vocab_flip(stat, 2), partner(stat)
    )
    partner_peak = p_stat[0]
    stat = jnp.stack([*merged(stat, came), *merged(p_stat, p_came)])
    small2, turned = after((third[1], rows), stat)
    came, sent2 = together([dp_flip(stat, k) for k in (3, 2, 1)], partner(small2))
    sent = (sent0, sent1, sent2)
    stat = combine(stat, *came)
    turned = after(turned, stat)
    came, other0 = together([dp_flip(stat, 4 * k) for k in (3, 2, 1)], flip(*turned[:2]))
    stat = combine(stat, *came)
    turned = after(turned[2:], stat)
    came, other1 = together(dp_flip(stat, 16), flip(*turned[:2]))
    own_factor, partner_factor = factors(table, share, stat, came, own_peak, partner_peak)

    def gradient(lines, exps, sent):
        own, other = (jnp.concatenate([f[g] for g in lines])[:, None] for f in (own_factor, partner_factor))
        onehot = column_ids[None, :] == jnp.concatenate([ids[g] for g in lines])[:, None]
        return (exps * own - onehot.astype(F32) - sent.astype(F32) * other).astype(BF16)

    def product(grad):
        return GRAD_SCALE * lax.dot_general(
            grad, both, (((1,), (1,)), ((), ())), preferred_element_type=F32
        )

    def wider(value):
        return value.astype(F32)

    def only(which, value):
        return jnp.where(core == which, value.astype(F32), 0.0)

    grad3 = gradient((3,), third[0], sent[2])
    p_last, turned = together(product(grad3), turned[2:])
    far = p_last[64:].astype(F16)
    c1 = ring(far, LARGE, -1)
    grad012 = after(jnp.concatenate([gradient((0, 1), exps0, sent[0]), gradient((2,), exps1, sent[1])], 0), far)
    p_rest = product(grad012)
    grads = [grad012, grad3]
    c1, p_rest, other2 = together(c1, p_rest, flip(*turned))
    rows_other = [*other0, *other1, *other2]
    p_near, p_up1, p_down1, p_up2, p_far2, p_up3 = (p_rest[64 * i : 64 * i + 64] for i in range(6))

    def step(up, down, cores=(0, 1)):
        up, down = together(up.astype(F16), down.astype(F16))
        return ring(up, LARGE, -1), ring(down, LARGE, 1, cores)

    def pass_on(value, step, cores=(0, 1)):
        return ring(value.astype(F16), SMALL, step, cores)

    c2u, c2d = step(p_up3 + wider(c1), p_last[:64])
    grads_other = [vocab_flip(g[:, columns:], 1) for g in grads]
    head_operands = [*rows, *rows_other], [*grads, *grads_other], columns
    grad_head = head(*head_operands, 0, 2)
    c2u, c2d, grad_head = together(c2u, c2d, grad_head)
    p_far2 = p_far2 + wider(c2d) + only(1, c2u)
    c3u, c3d = step(p_up2 + only(0, c2u), p_far2, (0,))
    p_wide = p_far2.reshape(4, 16, 4096)
    e1, e2d = pass_on(p_wide[1], -1, (1,)), pass_on(p_wide[3], 1, (1,))
    grad_head = head(*head_operands, 2, 3, grad_head)
    c3u, c3d, e1, e2d, grad_head = together(c3u, c3d, e1, e2d, grad_head)
    c4u, c4d = step(p_up1 + wider(c3u), p_down1 + wider(c3d))
    e2u = pass_on(p_wide[0] + wider(e1), -1, (1,))
    e3d = pass_on(p_wide[2] + wider(e2d), 1, (1,))
    grad_head = head(*head_operands, 5, 3, grad_head)
    c4u, c4d, e2u, e3d, grad_head = together(c4u, c4d, e2u, e3d, grad_head)
    p_near = (p_near + wider(c4u) + wider(c4d)).reshape(4, 16, 4096)
    e3u, e4d, e4u = together(
        pass_on(p_near[2] + wider(e2u), -2),
        pass_on(p_near[3] + wider(e3d), 1),
        pass_on(p_near[1], -1),
    )
    total = p_near[0] + wider(e4u) + wider(e4d) + wider(e3u)

    low, high = total[:, :2048], total[:, 2048:]
    came = vocab_flip(jnp.where(vocab < 2, high, low).astype(F16), 2).astype(F32)
    total = jnp.where(vocab < 2, low, high) + came
    low, high = total[:, :1024], total[:, 1024:]
    came = vocab_flip(jnp.where(core == 0, high, low), 1)
    grad_hidden = jnp.concatenate(
        [jnp.where(core == 0, low, came), jnp.where(core == 0, came, high)], 0
    ) * (1.0 / GRAD_SCALE)
    return (grad_hidden[None], grad_head[None])


def solution(mesh):
    placed = (P("mp", "dp", None), P("mp", None, ("dp", "vocab")), P(), P())
    return jax.shard_map(
        per_device,
        mesh=mesh,
        in_specs=placed,
        out_specs=(P("mp", "dp", "vocab"), P("mp", None, ("dp", "vocab"))),
        check_vma=False,
    )
```

```python
import jax
import jax.numpy as jnp
import numpy as np
from jax import lax
from jax.experimental import pallas as pl
from jax.experimental.pallas import tpu as pltpu
from jax.sharding import PartitionSpec as P

WARMUP = 1000
Z, X = 8, 4
F16 = jnp.float16
F32 = jnp.float32
BF16 = jnp.bfloat16
PROB_SCALE = 2.0**15
GRAD_SCALE = 2.0**14


def row_tables():
    near, wide = (0, -1, -2, 1), (-3, -4, 2, 3)
    along_z = (0, -1, 1, -2, 2, -3, 3, -4)
    along_x = ((near, 0), (near, -1), (near, 1), (near, -2), (wide, 0), (wide, -1), (wide, 1), (wide, -2))
    table = np.zeros((2, Z * X, 32), np.int32)
    for z in range(Z):
        for x in range(X):
            for i in range(8):
                for j in range(4):
                    at = i * 4 + j
                    table[0, z * X + x, at] = (z + along_z[i]) % Z * X + (x + near[j]) % X
                    offsets, shift = along_x[i]
                    table[1, z * X + x, at] = (z + offsets[j]) % Z * X + (x + shift) % X
    return table, np.argsort(table, axis=-1).astype(np.int32)


def ring(value, axes, step, cores=(0, 1)):
    pairs = []
    for z in range(Z):
        for x in range(X):
            for v in range(4):
                if v % 2 in cores:
                    if axes[v % 2] == "z":
                        to = (z + step) % Z * X + x
                    else:
                        to = z * X + (x + step) % X
                    pairs.append(((z * X + x) * 4 + v, to * 4 + v))
    return lax.ppermute(value, ("dp", "vocab"), pairs)


SMALL, LARGE = ("x", "z"), ("z", "x")


def dp_flip(value, mask):
    return lax.ppermute(value, "dp", [(i, i ^ mask) for i in range(Z * X)])


def vocab_flip(value, mask):
    return lax.ppermute(value, "vocab", [(v, v ^ mask) for v in range(4)])


def partner(value):
    return lax.ppermute(value, "mp", [(0, 1), (1, 0)])


def partner_vocab_flip(value, mask):
    pairs = [
        ((m * Z * X + i) * 4 + v, ((1 - m) * Z * X + i) * 4 + (v ^ mask))
        for m in range(2)
        for i in range(Z * X)
        for v in range(4)
    ]
    return lax.ppermute(value, ("mp", "dp", "vocab"), pairs)


def reordered(place, ref):
    piece = lax.broadcasted_iota(jnp.int32, (1, 128), 1) >> 4
    rows = []
    for r in range(4):
        row = jnp.zeros((1, 128), ref.dtype)
        for c in range(8):
            at = place(r * 8 + c)
            value = pltpu.roll(ref[pl.ds(at >> 3, 1), :], ((c - (at & 7)) & 7) * 16, 1)
            row = jnp.where(piece == c, value, row)
        rows.append(row)
    return rows


def ids_kernel(table, core, source, out):
    for r, row in enumerate(reordered(lambda p: 2 * table[p] + core[0], source)):
        out[r : r + 1, :] = row


def local_ids(table, core, targets):
    smem, vmem = pl.BlockSpec(memory_space=pltpu.SMEM), pl.BlockSpec(memory_space=pltpu.VMEM)
    return pl.pallas_call(
        ids_kernel,
        in_specs=[smem, smem, vmem],
        out_shape=jax.ShapeDtypeStruct((4, 128), jnp.int32),
    )(table, core.reshape(1), targets.reshape(8, 128))


def stat_kernel(table, *refs):
    out, held = refs[-2:]
    for which in range(2):
        at = 0
        for lines in refs[:-2]:
            for i in range(lines.shape[0]):
                held[at : at + 1, :] = lines[i, which : which + 1, :]
                at += 1
        for r, row in enumerate(reordered(lambda p: table[32 + p], held)):
            out[which, r : r + 1, :] = row


def statistics(table, lines):
    smem, vmem = pl.BlockSpec(memory_space=pltpu.SMEM), pl.BlockSpec(memory_space=pltpu.VMEM)
    return pl.pallas_call(
        stat_kernel,
        in_specs=[smem] + [vmem] * len(lines),
        out_shape=jax.ShapeDtypeStruct((2, 4, 128), F32),
        scratch_shapes=[pltpu.VMEM((4, 128), F32)],
    )(table, *lines)


def merged(*stats):
    peak = stats[0][0]
    for stat in stats[1:]:
        peak = jnp.maximum(peak, stat[0])
    return peak, sum(stat[1] * jnp.exp(stat[0] - peak) for stat in stats)


def combine(*stats):
    return jnp.stack([*merged(*[s[:2] for s in stats]), *merged(*[s[2:] for s in stats])])


def factor_kernel(table, share_ref, stat, came, own_peak, partner_peak, *refs):
    share = share_ref[0]
    held = refs[-1]
    for which, weight, peak in (
        (0, 1.0 + share, own_peak),
        (1, share * (1.0 / PROB_SCALE), partner_peak),
    ):
        first = 2 * which
        top, total = merged((stat[first], stat[first + 1]), (came[first], came[first + 1]))
        held[...] = weight * (jnp.exp(peak[...] - top) / total)
        for r, row in enumerate(reordered(lambda p: table[p], held)):
            refs[which * 2 + r // 2][:, r % 2 * 128 : r % 2 * 128 + 128] = row


def factors(table, share, *stats):
    smem, vmem = pl.BlockSpec(memory_space=pltpu.SMEM), pl.BlockSpec(memory_space=pltpu.VMEM)
    out = pl.pallas_call(
        factor_kernel,
        in_specs=[smem, smem] + [vmem] * 4,
        out_shape=(jax.ShapeDtypeStruct((1, 256), F32),) * 4,
        scratch_shapes=[pltpu.VMEM((4, 128), F32)],
    )(table, share.reshape(1), *stats)
    out = [v.reshape(256, 1) for v in out]
    return out[:2], out[2:]


def score_kernel(n, *refs):
    own, other, exps, lines, logits, held, done = refs[n:]
    steps, _, tile, columns = held.shape
    copies = [
        [
            pltpu.make_async_copy(w.at[pl.ds(k * tile, tile), :], held.at[k, side], done.at[k, side])
            for side, w in enumerate((own, other))
        ]
        for k in range(steps)
    ]
    for pair in copies:
        for copy in pair:
            copy.start()
    for k in range(steps):
        rows = jnp.concatenate([r[:, k * tile : (k + 1) * tile] for r in refs[:n]], 0)
        for side in range(2):
            copies[k][side].wait()
            part = jnp.dot(rows, held[k, side], preferred_element_type=F32)
            at = pl.ds(side * columns, columns)
            if k == 0:
                logits[:, at] = part
            else:
                logits[:, at] += part
    for i in range(n // 2):
        at = pl.ds(i * 128, 128)
        peak = jnp.max(logits[at, :], axis=1, keepdims=True)
        value = jnp.exp(logits[at, :] - peak)
        exps[at, :] = value
        total = jnp.sum(value, axis=1, keepdims=True)
        for which, column in enumerate((peak, total)):
            lines[i, which : which + 1, :] = jnp.broadcast_to(column, (128, 128)).T[:1]


def score(blocks, own, other, tile=1024):
    features, columns = own.shape
    n = len(blocks)
    vmem, hbm = pl.BlockSpec(memory_space=pltpu.VMEM), pl.BlockSpec(memory_space=pltpu.HBM)
    return pl.pallas_call(
        lambda *refs: score_kernel(n, *refs),
        in_specs=[vmem] * n + [hbm, hbm],
        out_specs=(vmem, vmem),
        out_shape=(
            jax.ShapeDtypeStruct((64 * n, 2 * columns), F32),
            jax.ShapeDtypeStruct((n // 2, 2, 128), F32),
        ),
        scratch_shapes=[
            pltpu.VMEM((64 * n, 2 * columns), F32),
            pltpu.VMEM((features // tile, 2, tile, columns), BF16),
            pltpu.SemaphoreType.DMA((features // tile, 2)),
        ],
        compiler_params=pltpu.CompilerParams(vmem_limit_bytes=20 * 2**20),
        cost_estimate=pl.CostEstimate(flops=1000, bytes_accessed=1000, transcendentals=0),
    )(*blocks, own, other)


def head_kernel(n, *refs):
    out, held = refs[-2:]

    @pl.when(pl.program_id(0) == 0)
    def _():
        at = 0
        for grad in refs[n:-2]:
            held[at : at + grad.shape[0], :] = grad[...]
            at += grad.shape[0]

    rows = jnp.concatenate([r[...] for r in refs[:n]], 0)
    out[...] = lax.dot_general(
        rows, held[...], (((0,), (0,)), ((), ())), preferred_element_type=F32
    )


def head(rows, grads, columns, first, steps, before=None, tile=512):
    features = rows[0].shape[1]
    total = sum(r.shape[0] for r in rows)
    earlier = [] if before is None else [before]

    def kernel(*refs):
        head_kernel(len(rows), *refs[: len(rows) + len(grads)], *refs[-2:])

    return pl.pallas_call(
        kernel,
        grid=(steps,),
        in_specs=[pl.BlockSpec((r.shape[0], tile), lambda i: (0, first + i)) for r in rows]
        + [pl.BlockSpec((g.shape[0], columns), lambda i: (0, 0)) for g in grads]
        + [pl.BlockSpec(memory_space=pl.ANY)] * len(earlier),
        out_specs=pl.BlockSpec((tile, columns), lambda i: (first + i, 0)),
        out_shape=jax.ShapeDtypeStruct((features, columns), F32),
        scratch_shapes=[pltpu.VMEM((total, columns), BF16)],
        input_output_aliases={len(rows) + len(grads): 0} if earlier else {},
        compiler_params=pltpu.CompilerParams(vmem_limit_bytes=50 * 2**20),
        cost_estimate=pl.CostEstimate(flops=1000, bytes_accessed=1000, transcendentals=0),
    )(*rows, *grads, *earlier)


def after(value, *earlier):
    return lax.optimization_barrier((value, *earlier))[0]


def together(*values):
    return lax.optimization_barrier(values)


def per_device(hidden_states, head_weight, targets, train_step):
    hidden = hidden_states[0]
    weight = head_weight[0]
    columns = weight.shape[1]
    vocab = lax.axis_index("vocab")
    dp = lax.axis_index("dp")
    core = vocab % 2
    share = 0.5 * jnp.minimum(train_step[0].astype(F32) / WARMUP, 1.0)
    mine = lax.dynamic_slice_in_dim(hidden, core * 16, 16, 0)
    weight_other = vocab_flip(weight, 1)
    u2, d1, u1 = together(ring(mine, SMALL, 2), ring(mine, SMALL, -1), ring(mine, SMALL, 1))
    near = jnp.concatenate([mine, u1, u2, d1], 0)
    up1, down1 = ring(near, LARGE, 1), ring(near, LARGE, -1)
    targets, place, d1 = after((targets, core * 32 + dp, d1), near)
    table = jnp.asarray(np.concatenate([t.reshape(64, 32) for t in row_tables()], 1))
    table = lax.dynamic_index_in_dim(table, place, 0, keepdims=False)
    ids = local_ids(table, core, targets).reshape(512)
    u3, d2 = together(ring(u2, SMALL, 1, (1,)), ring(d1, SMALL, -1, (1,)))
    up1, down1, u3, d2, weight_other, ids, table = together(
        up1, down1, u3, d2, weight_other, ids, table
    )

    both = jnp.concatenate([weight, weight_other], 1)
    column_ids = jnp.concatenate(
        [(dp * 4 + v) * columns + lax.iota(jnp.int32, columns) for v in (vocab, vocab ^ 1)]
    )

    def scores(*blocks):
        exps, lines = score(blocks, weight, weight_other)
        return exps, (exps * PROB_SCALE).astype(F16), lines

    def flip(*blocks):
        return [vocab_flip(b, 1) for b in blocks]

    up2, down2 = ring(up1, LARGE, 1), ring(down1, LARGE, -1, (0,))
    u4, d3 = ring(u3, SMALL, 1, (1,)), ring(d2, SMALL, -1, (1,))
    up2, down2, u4, d3, weight_other = together(up2, down2, u4, d3, weight_other)
    wide = jnp.concatenate([u3, u4, d2, d3], 0)
    far2 = jnp.where(core == 0, down2, wide)
    turn = jnp.where(core == 0, up2, wide)
    up3, down3 = ring(turn, LARGE, 1), ring(far2, LARGE, -1)
    far = ring(turn[:32], LARGE, 2), ring(far2[32:], LARGE, -2)
    first = scores(near, up1, down1, up2)
    up3, down3, far, exps0 = together(up3, down3, far, first[0])
    far = jnp.concatenate(far, 0)
    second = scores(far2, up3, down3, far)
    lines, sent0 = after((second[2], partner(first[1])), second[0])
    rows = [near, up1, down1, up2, far2, up3, down3, far]

    stat = statistics(table, (first[2], lines))
    own_peak = stat[0]
    came, p_came, p_stat = together(
        vocab_flip(stat, 2), partner_vocab_flip(stat, 2), partner(stat)
    )
    partner_peak = p_stat[0]
    stat = jnp.stack([*merged(stat, came), *merged(p_stat, p_came)])
    small, turned = after((second[1], rows), stat)
    sent1 = partner(small)
    came, other0 = together([dp_flip(stat, k) for k in (3, 2, 1)], flip(turned[0]))
    stat = combine(stat, *came)
    turned = after(turned[1:], stat)
    came, other1 = together([dp_flip(stat, 4 * k) for k in (3, 2, 1)], flip(turned[0]))
    stat = combine(stat, *came)
    turned = after(turned[1:], stat)
    came, other2 = together(dp_flip(stat, 16), flip(*turned[:3]))
    own_factor, partner_factor = factors(table, share, stat, came, own_peak, partner_peak)

    def gradient(g, exps, sent):
        onehot = column_ids[None, :] == ids[256 * g : 256 * g + 256][:, None]
        grad = exps * own_factor[g] - onehot.astype(F32)
        return (grad - sent.astype(F32) * partner_factor[g]).astype(BF16)

    def product(grad):
        return GRAD_SCALE * lax.dot_general(
            grad, both, (((1,), (1,)), ((), ())), preferred_element_type=F32
        )

    def wider(value):
        return value.astype(F32)

    def only(which, value):
        return jnp.where(core == which, value.astype(F32), 0.0)

    grad1 = gradient(1, second[0], sent1)
    p_far, other3, grad1_other = together(
        product(grad1), flip(*after(turned[3:], own_factor[1])), vocab_flip(grad1[:, columns:], 1)
    )
    rows_other = [*other0, *other1, *other2, *other3]
    p_far2, p_up3, p_down3, p_far = (p_far[64 * i : 64 * i + 64] for i in range(4))

    def step(up, down, cores=(0, 1)):
        up, down = together(up.astype(F16), down.astype(F16))
        return ring(up, LARGE, -1), ring(down, LARGE, 1, cores)

    def pass_on(value, step, cores=(0, 1)):
        return ring(value.astype(F16), SMALL, step, cores)

    pay2u, pay2d, far_low, far_high = together(
        *[p.astype(F16) for p in (p_up3, p_down3, p_far[:32], p_far[32:])]
    )
    c2u, c2d = ring(pay2u, LARGE, -1), ring(pay2d, LARGE, 1)
    far_low, far_high = ring(far_low, LARGE, -2), ring(far_high, LARGE, 2)
    grad0 = after(gradient(0, exps0, sent0), pay2u)
    p_rest = product(grad0)
    grads = [grad0, grad1, vocab_flip(grad0[:, columns:], 1), grad1_other]
    head_operands = [*rows, *rows_other], grads, columns
    grad_head = head(*head_operands, 0, 2)
    c2u, c2d, far_low, far_high, p_rest, grad_head = together(
        c2u, c2d, far_low, far_high, p_rest, grad_head
    )
    p_near, p_up1, p_down1, p_up2 = (p_rest[64 * i : 64 * i + 64] for i in range(4))
    p_up2 = jnp.concatenate([p_up2[:32] + only(0, far_low), p_up2[32:]], 0)
    p_far2 = p_far2 + jnp.concatenate([only(1, far_low), wider(far_high)], 0)
    p_far2 = p_far2 + wider(c2d) + only(1, c2u)
    c3u, c3d = step(p_up2 + only(0, c2u), p_far2, (0,))
    p_wide = p_far2.reshape(4, 16, 4096)
    e1, e2d = pass_on(p_wide[1], -1, (1,)), pass_on(p_wide[3], 1, (1,))
    grad_head = head(*head_operands, 2, 3, grad_head)
    c3u, c3d, e1, e2d, grad_head = together(c3u, c3d, e1, e2d, grad_head)
    c4u, c4d = step(p_up1 + wider(c3u), p_down1 + wider(c3d))
    e2u = pass_on(p_wide[0] + wider(e1), -1, (1,))
    e3d = pass_on(p_wide[2] + wider(e2d), 1, (1,))
    grad_head = head(*head_operands, 5, 3, grad_head)
    c4u, c4d, e2u, e3d, grad_head = together(c4u, c4d, e2u, e3d, grad_head)
    p_near = (p_near + wider(c4u) + wider(c4d)).reshape(4, 16, 4096)
    e3u, e4d, e4u = together(
        pass_on(p_near[2] + wider(e2u), -2),
        pass_on(p_near[3] + wider(e3d), 1),
        pass_on(p_near[1], -1),
    )
    total = p_near[0] + wider(e4u) + wider(e4d) + wider(e3u)

    low, high = total[:, :2048], total[:, 2048:]
    came = vocab_flip(jnp.where(vocab < 2, high, low).astype(F16), 2).astype(F32)
    total = jnp.where(vocab < 2, low, high) + came
    low, high = total[:, :1024], total[:, 1024:]
    came = vocab_flip(jnp.where(core == 0, high, low), 1)
    grad_hidden = jnp.concatenate(
        [jnp.where(core == 0, low, came), jnp.where(core == 0, came, high)], 0
    ) * (1.0 / GRAD_SCALE)
    return (grad_hidden[None], grad_head[None])


def solution(mesh):
    placed = (P("mp", "dp", None), P("mp", None, ("dp", "vocab")), P(), P())
    return jax.shard_map(
        per_device,
        mesh=mesh,
        in_specs=placed,
        out_specs=(P("mp", "dp", "vocab"), P("mp", None, ("dp", "vocab"))),
        check_vma=False,
    )
```

```python
import jax
import jax.numpy as jnp
import numpy as np
from jax import lax
from jax.experimental import pallas as pl
from jax.experimental.pallas import tpu as pltpu
from jax.sharding import PartitionSpec as P

WARMUP = 1000
Z, X = 8, 4
F16 = jnp.float16
F32 = jnp.float32
BF16 = jnp.bfloat16
PROB_SCALE = 2.0**15
GRAD_SCALE = 2.0**14


def row_tables():
    near, wide = (0, -1, -2, 1), (-3, -4, 2, 3)
    along_z = (0, -1, 1, -2, 2, -3, 3, -4)
    along_x = ((near, 0), (near, -1), (near, 1), (near, -2), (wide, 0), (wide, -1), (wide, 1), (wide, -2))
    table = np.zeros((2, Z * X, 32), np.int32)
    for z in range(Z):
        for x in range(X):
            for i in range(8):
                for j in range(4):
                    at = i * 4 + j
                    table[0, z * X + x, at] = (z + along_z[i]) % Z * X + (x + near[j]) % X
                    offsets, shift = along_x[i]
                    table[1, z * X + x, at] = (z + offsets[j]) % Z * X + (x + shift) % X
    return table, np.argsort(table, axis=-1).astype(np.int32)


def ring(value, axes, step, cores=(0, 1)):
    pairs = []
    for z in range(Z):
        for x in range(X):
            for v in range(4):
                if v % 2 in cores:
                    if axes[v % 2] == "z":
                        to = (z + step) % Z * X + x
                    else:
                        to = z * X + (x + step) % X
                    pairs.append(((z * X + x) * 4 + v, to * 4 + v))
    return lax.ppermute(value, ("dp", "vocab"), pairs)


SMALL, LARGE = ("x", "z"), ("z", "x")


def dp_flip(value, mask):
    return lax.ppermute(value, "dp", [(i, i ^ mask) for i in range(Z * X)])


def vocab_flip(value, mask):
    return lax.ppermute(value, "vocab", [(v, v ^ mask) for v in range(4)])


def partner(value):
    return lax.ppermute(value, "mp", [(0, 1), (1, 0)])


def partner_vocab_flip(value, mask):
    pairs = [
        ((m * Z * X + i) * 4 + v, ((1 - m) * Z * X + i) * 4 + (v ^ mask))
        for m in range(2)
        for i in range(Z * X)
        for v in range(4)
    ]
    return lax.ppermute(value, ("mp", "dp", "vocab"), pairs)


def reordered(place, ref):
    piece = lax.broadcasted_iota(jnp.int32, (1, 128), 1) >> 4
    rows = []
    for r in range(4):
        row = jnp.zeros((1, 128), ref.dtype)
        for c in range(8):
            at = place(r * 8 + c)
            value = pltpu.roll(ref[pl.ds(at >> 3, 1), :], ((c - (at & 7)) & 7) * 16, 1)
            row = jnp.where(piece == c, value, row)
        rows.append(row)
    return rows


def ids_kernel(table, core, source, out):
    for r, row in enumerate(reordered(lambda p: 2 * table[p] + core[0], source)):
        out[r : r + 1, :] = row


def local_ids(table, core, targets):
    smem, vmem = pl.BlockSpec(memory_space=pltpu.SMEM), pl.BlockSpec(memory_space=pltpu.VMEM)
    return pl.pallas_call(
        ids_kernel,
        in_specs=[smem, smem, vmem],
        out_shape=jax.ShapeDtypeStruct((4, 128), jnp.int32),
    )(table, core.reshape(1), targets.reshape(8, 128))


def stat_kernel(table, *refs):
    out, held = refs[-2:]
    for which in range(2):
        at = 0
        for lines in refs[:-2]:
            for i in range(lines.shape[0]):
                held[at : at + 1, :] = lines[i, which : which + 1, :]
                at += 1
        for r, row in enumerate(reordered(lambda p: table[32 + p], held)):
            out[which, r : r + 1, :] = row


def statistics(table, lines):
    smem, vmem = pl.BlockSpec(memory_space=pltpu.SMEM), pl.BlockSpec(memory_space=pltpu.VMEM)
    return pl.pallas_call(
        stat_kernel,
        in_specs=[smem] + [vmem] * len(lines),
        out_shape=jax.ShapeDtypeStruct((2, 4, 128), F32),
        scratch_shapes=[pltpu.VMEM((4, 128), F32)],
    )(table, *lines)


def merged(*stats):
    peak = stats[0][0]
    for stat in stats[1:]:
        peak = jnp.maximum(peak, stat[0])
    return peak, sum(stat[1] * jnp.exp(stat[0] - peak) for stat in stats)


def combine(*stats):
    return jnp.stack([*merged(*[s[:2] for s in stats]), *merged(*[s[2:] for s in stats])])


def factor_kernel(table, share_ref, stat, came, own_peak, partner_peak, *refs):
    share = share_ref[0]
    held = refs[-1]
    for which, weight, peak in (
        (0, 1.0 + share, own_peak),
        (1, share * (1.0 / PROB_SCALE), partner_peak),
    ):
        first = 2 * which
        top, total = merged((stat[first], stat[first + 1]), (came[first], came[first + 1]))
        held[...] = weight * (jnp.exp(peak[...] - top) / total)
        for r, row in enumerate(reordered(lambda p: table[p], held)):
            refs[which * 2 + r // 2][:, r % 2 * 128 : r % 2 * 128 + 128] = row


def factors(table, share, *stats):
    smem, vmem = pl.BlockSpec(memory_space=pltpu.SMEM), pl.BlockSpec(memory_space=pltpu.VMEM)
    out = pl.pallas_call(
        factor_kernel,
        in_specs=[smem, smem] + [vmem] * 4,
        out_shape=(jax.ShapeDtypeStruct((1, 256), F32),) * 4,
        scratch_shapes=[pltpu.VMEM((4, 128), F32)],
    )(table, share.reshape(1), *stats)
    out = [v.reshape(256, 1) for v in out]
    return out[:2], out[2:]


def score_kernel(n, *refs):
    own, other, exps, lines, logits, held, done = refs[n:]
    steps, _, tile, columns = held.shape
    copies = [
        [
            pltpu.make_async_copy(w.at[pl.ds(k * tile, tile), :], held.at[k, side], done.at[k, side])
            for side, w in enumerate((own, other))
        ]
        for k in range(steps)
    ]
    for pair in copies:
        for copy in pair:
            copy.start()
    for k in range(steps):
        rows = jnp.concatenate([r[:, k * tile : (k + 1) * tile] for r in refs[:n]], 0)
        for side in range(2):
            copies[k][side].wait()
            part = jnp.dot(rows, held[k, side], preferred_element_type=F32)
            at = pl.ds(side * columns, columns)
            if k == 0:
                logits[:, at] = part
            else:
                logits[:, at] += part
    for i in range(n // 2):
        at = pl.ds(i * 128, 128)
        peak = jnp.max(logits[at, :], axis=1, keepdims=True)
        value = jnp.exp(logits[at, :] - peak)
        exps[at, :] = value
        total = jnp.sum(value, axis=1, keepdims=True)
        for which, column in enumerate((peak, total)):
            lines[i, which : which + 1, :] = jnp.broadcast_to(column, (128, 128)).T[:1]


def score(blocks, own, other, tile=1024):
    features, columns = own.shape
    n = len(blocks)
    vmem, hbm = pl.BlockSpec(memory_space=pltpu.VMEM), pl.BlockSpec(memory_space=pltpu.HBM)
    return pl.pallas_call(
        lambda *refs: score_kernel(n, *refs),
        in_specs=[vmem] * n + [hbm, hbm],
        out_specs=(vmem, vmem),
        out_shape=(
            jax.ShapeDtypeStruct((64 * n, 2 * columns), F32),
            jax.ShapeDtypeStruct((n // 2, 2, 128), F32),
        ),
        scratch_shapes=[
            pltpu.VMEM((64 * n, 2 * columns), F32),
            pltpu.VMEM((features // tile, 2, tile, columns), BF16),
            pltpu.SemaphoreType.DMA((features // tile, 2)),
        ],
        compiler_params=pltpu.CompilerParams(vmem_limit_bytes=20 * 2**20),
        cost_estimate=pl.CostEstimate(flops=1000, bytes_accessed=1000, transcendentals=0),
    )(*blocks, own, other)


def head_kernel(n, *refs):
    out, held = refs[-2:]

    @pl.when(pl.program_id(0) == 0)
    def _():
        at = 0
        for grad in refs[n:-2]:
            held[at : at + grad.shape[0], :] = grad[...]
            at += grad.shape[0]

    rows = jnp.concatenate([r[...] for r in refs[:n]], 0)
    out[...] = lax.dot_general(
        rows, held[...], (((0,), (0,)), ((), ())), preferred_element_type=F32
    )


def head(rows, grads, columns, first, steps, before=None, tile=512):
    features = rows[0].shape[1]
    total = sum(r.shape[0] for r in rows)
    earlier = [] if before is None else [before]

    def kernel(*refs):
        head_kernel(len(rows), *refs[: len(rows) + len(grads)], *refs[-2:])

    return pl.pallas_call(
        kernel,
        grid=(steps,),
        in_specs=[pl.BlockSpec((r.shape[0], tile), lambda i: (0, first + i)) for r in rows]
        + [pl.BlockSpec((g.shape[0], columns), lambda i: (0, 0)) for g in grads]
        + [pl.BlockSpec(memory_space=pl.ANY)] * len(earlier),
        out_specs=pl.BlockSpec((tile, columns), lambda i: (first + i, 0)),
        out_shape=jax.ShapeDtypeStruct((features, columns), F32),
        scratch_shapes=[pltpu.VMEM((total, columns), BF16)],
        input_output_aliases={len(rows) + len(grads): 0} if earlier else {},
        compiler_params=pltpu.CompilerParams(vmem_limit_bytes=50 * 2**20),
        cost_estimate=pl.CostEstimate(flops=1000, bytes_accessed=1000, transcendentals=0),
    )(*rows, *grads, *earlier)


def after(value, *earlier):
    return lax.optimization_barrier((value, *earlier))[0]


def together(*values):
    return lax.optimization_barrier(values)


def per_device(hidden_states, head_weight, targets, train_step):
    hidden = hidden_states[0]
    weight = head_weight[0]
    columns = weight.shape[1]
    vocab = lax.axis_index("vocab")
    dp = lax.axis_index("dp")
    core = vocab % 2
    share = 0.5 * jnp.minimum(train_step[0].astype(F32) / WARMUP, 1.0)
    mine = lax.dynamic_slice_in_dim(hidden, core * 16, 16, 0)
    weight_other = vocab_flip(weight, 1)
    u2, d1, u1 = together(ring(mine, SMALL, 2), ring(mine, SMALL, -1), ring(mine, SMALL, 1))
    near = jnp.concatenate([mine, u1, u2, d1], 0)
    up1, down1 = ring(near, LARGE, 1), ring(near, LARGE, -1)
    targets, place, d1 = after((targets, core * 32 + dp, d1), near)
    table = jnp.asarray(np.concatenate([t.reshape(64, 32) for t in row_tables()], 1))
    table = lax.dynamic_index_in_dim(table, place, 0, keepdims=False)
    ids = local_ids(table, core, targets).reshape(512)
    u3, d2 = together(ring(u2, SMALL, 1, (1,)), ring(d1, SMALL, -1, (1,)))
    up1, down1, u3, d2, weight_other, ids, table = together(
        up1, down1, u3, d2, weight_other, ids, table
    )

    both = jnp.concatenate([weight, weight_other], 1)
    column_ids = jnp.concatenate(
        [(dp * 4 + v) * columns + lax.iota(jnp.int32, columns) for v in (vocab, vocab ^ 1)]
    )

    def scores(*blocks):
        exps, lines = score(blocks, weight, weight_other)
        return exps, (exps * PROB_SCALE).astype(F16), lines

    def flip(*blocks):
        return [vocab_flip(b, 1) for b in blocks]

    up2, down2 = ring(up1, LARGE, 1), ring(down1, LARGE, -1, (0,))
    u4, d3 = ring(u3, SMALL, 1, (1,)), ring(d2, SMALL, -1, (1,))
    up2, down2, u4, d3, weight_other = together(up2, down2, u4, d3, weight_other)
    wide = jnp.concatenate([u3, u4, d2, d3], 0)
    far2 = jnp.where(core == 0, down2, wide)
    turn = jnp.where(core == 0, up2, wide)
    up3, down3 = ring(turn, LARGE, 1), ring(far2, LARGE, -1)
    far = ring(turn[:32], LARGE, 2), ring(far2[32:], LARGE, -2)
    first = scores(near, up1, down1, up2)
    up3, down3, far, exps0 = together(up3, down3, far, first[0])
    far = jnp.concatenate(far, 0)
    second = scores(far2, up3, down3, far)
    lines, sent0 = after((second[2], partner(first[1])), second[0])
    rows = [near, up1, down1, up2, far2, up3, down3, far]

    stat = statistics(table, (first[2], lines))
    own_peak = stat[0]
    came, p_came, p_stat = together(
        vocab_flip(stat, 2), partner_vocab_flip(stat, 2), partner(stat)
    )
    partner_peak = p_stat[0]
    stat = jnp.stack([*merged(stat, came), *merged(p_stat, p_came)])
    small, turned = after((second[1], rows), stat)
    sent1 = partner(small)
    came, other0 = together([dp_flip(stat, k) for k in (3, 2, 1)], flip(turned[0]))
    stat = combine(stat, *came)
    turned = after(turned[1:], stat)
    came, other1 = together([dp_flip(stat, 4 * k) for k in (3, 2, 1)], flip(turned[0]))
    stat = combine(stat, *came)
    turned = after(turned[1:], stat)
    came, other2 = together(dp_flip(stat, 16), flip(*turned[:3]))
    own_factor, partner_factor = factors(table, share, stat, came, own_peak, partner_peak)

    def gradient(g, exps, sent):
        onehot = column_ids[None, :] == ids[256 * g : 256 * g + 256][:, None]
        grad = exps * own_factor[g] - onehot.astype(F32)
        return (grad - sent.astype(F32) * partner_factor[g]).astype(BF16)

    def product(grad):
        return GRAD_SCALE * lax.dot_general(
            grad, both, (((1,), (1,)), ((), ())), preferred_element_type=F32
        )

    def wider(value):
        return value.astype(F32)

    def only(which, value):
        return jnp.where(core == which, value.astype(F32), 0.0)

    grad1 = gradient(1, second[0], sent1)
    p_far, other3, grad1_other = together(
        product(grad1), flip(*after(turned[3:], own_factor[1])), vocab_flip(grad1[:, columns:], 1)
    )
    rows_other = [*other0, *other1, *other2, *other3]
    p_far2, p_up3, p_down3, p_far = (p_far[64 * i : 64 * i + 64] for i in range(4))

    def step(up, down, cores=(0, 1)):
        up, down = together(up.astype(F16), down.astype(F16))
        return ring(up, LARGE, -1), ring(down, LARGE, 1, cores)

    def pass_on(value, step, cores=(0, 1)):
        return ring(value.astype(F16), SMALL, step, cores)

    pay2u, pay2d, far_low, far_high = together(
        *[p.astype(F16) for p in (p_up3, p_down3, p_far[:32], p_far[32:])]
    )
    c2u, c2d = ring(pay2u, LARGE, -1), ring(pay2d, LARGE, 1)
    far_low, far_high = ring(far_low, LARGE, -2), ring(far_high, LARGE, 2)
    grad0 = after(gradient(0, exps0, sent0), pay2u)
    p_rest = product(grad0)
    grads = [grad0, grad1, vocab_flip(grad0[:, columns:], 1), grad1_other]
    head_operands = [*rows, *rows_other], grads, columns
    grad_head = head(*head_operands, 0, 2)
    c2u, c2d, far_low, far_high, p_rest, grad_head = together(
        c2u, c2d, far_low, far_high, p_rest, grad_head
    )
    p_near, p_up1, p_down1, p_up2 = (p_rest[64 * i : 64 * i + 64] for i in range(4))
    far = wider(jnp.concatenate([far_low, far_high], 0))
    low = lax.broadcasted_iota(jnp.int32, (64, 1), 0) < 32
    p_far2 = p_far2 + jnp.where(low & (core == 0), 0.0, far) + wider(c2d) + only(1, c2u)
    p_up2 = p_up2 + jnp.where(low & (core == 0), far, 0.0) + only(0, c2u)
    c3u, c3d = step(p_up2, p_far2, (0,))
    p_wide = p_far2.reshape(4, 16, 4096)
    e1, e2d = pass_on(p_wide[1], -1, (1,)), pass_on(p_wide[3], 1, (1,))
    grad_head = head(*head_operands, 2, 3, grad_head)
    c3u, c3d, e1, e2d, grad_head = together(c3u, c3d, e1, e2d, grad_head)
    c4u, c4d = step(p_up1 + wider(c3u), p_down1 + wider(c3d))
    e2u = pass_on(p_wide[0] + wider(e1), -1, (1,))
    e3d = pass_on(p_wide[2] + wider(e2d), 1, (1,))
    grad_head = head(*head_operands, 5, 3, grad_head)
    c4u, c4d, e2u, e3d, grad_head = together(c4u, c4d, e2u, e3d, grad_head)
    p_near = (p_near + wider(c4u) + wider(c4d)).reshape(4, 16, 4096)
    e3u, e4d, e4u = together(
        pass_on(p_near[2] + wider(e2u), -2),
        pass_on(p_near[3] + wider(e3d), 1),
        pass_on(p_near[1], -1),
    )
    total = p_near[0] + wider(e4u) + wider(e4d) + wider(e3u)

    low, high = total[:, :2048], total[:, 2048:]
    came = vocab_flip(jnp.where(vocab < 2, high, low).astype(F16), 2).astype(F32)
    total = jnp.where(vocab < 2, low, high) + came
    low, high = total[:, :1024], total[:, 1024:]
    came = vocab_flip(jnp.where(core == 0, high, low), 1)
    grad_hidden = jnp.concatenate(
        [jnp.where(core == 0, low, came), jnp.where(core == 0, came, high)], 0
    ) * (1.0 / GRAD_SCALE)
    return (grad_hidden[None], grad_head[None])


def solution(mesh):
    placed = (P("mp", "dp", None), P("mp", None, ("dp", "vocab")), P(), P())
    return jax.shard_map(
        per_device,
        mesh=mesh,
        in_specs=placed,
        out_specs=(P("mp", "dp", "vocab"), P("mp", None, ("dp", "vocab"))),
        check_vma=False,
    )
```
